32 devices in a mesh: space: 8 (over y, x, core), shell: 4 (over z).
Axes of the slice: x: 2, y: 2, z: 4, core: 2. Of those that a mesh axis runs over, the one named last changes fastest.
Arguments:
- weights: float32 [65536], P(('space', 'shell')), may hold values from 0.02 to 1.5
- seg_streamline: int32 [8, 4, 8, 256], P('space', 'shell'), may hold values from 0 to 2047
- seg_features: float32 [8, 4, 8, 256, 128], P('space', 'shell'), may hold values from -12 to 12
- pair_counts: int32 [8, 4, 8], P('space', 'shell'), may hold values from 32 to 256, as said below
- seg_voxel: int32 [8, 4, 8, 256], P('space', 'shell'), may hold values from 0 to 4095
- dictionary: float32 [128, 256], P(None, 'shell'), may hold values from -0.375 to 0.375
- measured: float32 [256, 32768], P('shell', 'space'), may hold values from -6 to 6
Outputs:
- new_weights: float32 [65536], P(('space', 'shell'))
- residual: float32 [256, 32768], P('shell', 'space')
The draws below stay inside these ranges and needn't reach their ends.
Inputs may be any that keep to these rules, and one draw needn't show every extreme that they name: In each shell group q one voxel block d has pair_counts[s, q, d] = 256 for every s.
All inputs are finite; a program needn't handle non-finite values.
Results may differ from the reference program's by a relative error of at most 0.0003.
Values sent between devices are 32-bit elements; how exact they have to be, the bound alone decides.
A program may use at most 64 MiB of HBM per device.

```python
import math
import jax
import jax.numpy as jnp
from jax import lax

DIRS = 256
COEFFS = 128
VOX_DEV = 4096
STR_DEV = 2048
CAP = 256
ITERS = 2
VBLOCKS = 8
SHELLS = 4
VOXELS = 32768
STREAMLINES = 65536


def draw_seg_features(key, part):
    key_base = jax.random.fold_in(key, 11)
    key_len = jax.random.fold_in(key, 12)
    key_col = jax.random.fold_in(key, 13)
    full_shape = (VBLOCKS, SHELLS, VBLOCKS, CAP, COEFFS)
    base_draw = jnp.clip(jax.random.normal(key_base, full_shape, jnp.float32), -4.0, 4.0)
    seglen = jnp.exp(jax.random.uniform(key_len, (VBLOCKS, SHELLS, VBLOCKS, CAP, 1), jnp.float32, math.log(0.1), math.log(2.0)))
    column = jnp.exp(jax.random.uniform(key_col, (COEFFS,), jnp.float32, math.log(0.3), math.log(3.0)))
    return 0.5 * base_draw * seglen * column


def draw_pair_counts(key, part):
    key_base = jax.random.fold_in(key, 21)
    key_hot = jax.random.fold_in(key, 22)
    base_draw = jax.random.randint(key_base, (VBLOCKS, SHELLS, VBLOCKS), max(1, CAP // 8), CAP // 2 + 1, jnp.int32)
    hot_block = jax.random.randint(key_hot, (SHELLS,), 0, VBLOCKS, jnp.int32)
    target = jnp.arange(VBLOCKS, dtype=jnp.int32)[None, None, :]
    return jnp.where(target == hot_block[None, :, None], jnp.int32(CAP), base_draw)


def touch_ends(result, stream_key, least, high):
    place = [jax.random.randint(jax.random.fold_in(stream_key, axis), (), 0, length) for axis, length in enumerate(result.shape)]
    main_axis = result.shape.index(max(result.shape))
    beside = place[:main_axis] + [(place[main_axis] + 1) % result.shape[main_axis]] + place[main_axis + 1:]
    return result.at[tuple(place)].set(least).at[tuple(beside)].set(high)


def shard_levels(own_key, shape, split, low, top_value):
    factor_of = 1.0
    for axis_at, shards_of in split:
        draws = jax.random.uniform(jax.random.fold_in(jax.random.fold_in(own_key, 6), axis_at), (shards_of,), jnp.float32, low / len(split), top_value / len(split))
        factor_of = factor_of * jnp.repeat(jnp.exp(draws), shape[axis_at] // shards_of).reshape((-1,) + (1,) * (len(shape) - 1 - axis_at))
    return factor_of


def scatter_about(rng, dims, scale, most, split=(), kind=jnp.bfloat16):
    result = jax.random.normal(rng, dims, jnp.float32) * scale
    if len(split) > 0:
        result = shard_levels(rng, dims, split, -0.22, 0.18) * result
    return jnp.clip(result, min=-most, max=most).astype(kind)


def setup_inputs(seed: int = 0) -> dict:
    streams_of = jax.random.split(jax.random.key(seed), 8)
    weights = jnp.clip(0.02 + 1.48 * jax.random.uniform(streams_of[0], (STREAMLINES,), jnp.float32) ** shard_levels(streams_of[0], (STREAMLINES,), ((0, 32),), -0.2, 0.2), 0.02, 1.5)
    seg_streamline = touch_ends(jax.random.randint(streams_of[1], (VBLOCKS, SHELLS, VBLOCKS, CAP), 0, STR_DEV), jax.random.fold_in(streams_of[1], 1), 0, STR_DEV - 1).astype(jnp.int32)
    seg_features = draw_seg_features(jax.random.fold_in(streams_of[7], 71), 0)
    pair_counts = draw_pair_counts(jax.random.fold_in(streams_of[7], 71), 0)
    seg_voxel = touch_ends(jax.random.randint(streams_of[4], (VBLOCKS, SHELLS, VBLOCKS, CAP), 0, VOX_DEV), jax.random.fold_in(streams_of[4], 1), 0, VOX_DEV - 1).astype(jnp.int32)
    dictionary = scatter_about(streams_of[5], (COEFFS, DIRS), DIRS ** -0.5, 0.375, ((1, 4),), jnp.float32)
    measured = scatter_about(streams_of[6], (DIRS, VOXELS), 1.0, 6.0, ((0, 4), (1, 8)), jnp.float32)
    return dict(weights=weights, seg_streamline=seg_streamline, seg_features=seg_features, pair_counts=pair_counts, seg_voxel=seg_voxel, dictionary=dictionary, measured=measured)


def reference(weights, seg_streamline, seg_features, pair_counts, seg_voxel, dictionary, measured):
    slot_pos = jnp.arange(CAP, dtype=jnp.int32)[None, None, None, :]
    live_slot = slot_pos < pair_counts[..., None]
    features = jnp.where(live_slot[..., None], seg_features, jnp.float32(0.0))
    source = jnp.arange(VBLOCKS, dtype=jnp.int32)[:, None, None, None]
    shell_pos = jnp.arange(SHELLS, dtype=jnp.int32)[None, :, None, None]
    target = jnp.arange(VBLOCKS, dtype=jnp.int32)[None, None, :, None]
    owner_index = ((source * SHELLS + shell_pos) * STR_DEV + seg_streamline).astype(jnp.int32)
    voxel_flat = (target * VOX_DEV + jnp.transpose(seg_voxel, (2, 1, 0, 3))).astype(jnp.int32)
    column_sq = jnp.zeros((STREAMLINES,), jnp.float32).at[owner_index].add(jnp.sum(features * features, axis=-1))
    scaling = 0.5 / (0.5 + column_sq)
    current = weights
    residual = jnp.zeros((DIRS, VOXELS), jnp.float32)
    for iteration in range(ITERS):
        seg_terms = current[owner_index][..., None] * features
        coeff = jnp.zeros((VOXELS, COEFFS), jnp.float32).at[voxel_flat].add(seg_terms)
        residual = jnp.einsum("jg,vj->gv", dictionary, coeff, precision=lax.Precision.HIGHEST) - measured
        adjoint = jnp.einsum("gv,jg->vj", residual, dictionary, precision=lax.Precision.HIGHEST)
        grad_slot = jnp.sum(features * adjoint[voxel_flat], axis=-1)
        gradient = jnp.zeros((STREAMLINES,), jnp.float32).at[owner_index].add(grad_slot)
        current = jnp.maximum(current - scaling * gradient, 0.0)
    return current, residual
```

```python
import functools

import jax
import jax.numpy as jnp
from jax import lax
from jax.experimental import pallas as pl
from jax.experimental.pallas import tpu as pltpu
from jax.sharding import PartitionSpec as P

ITERS = 2
LANES = 128
ROWS_STEP = 8
HIGH = lax.Precision.HIGHEST


def local_kernel(dirs, voxel_ref, x_ref, counts_ref, pairs_ref, start_ref, resid_ref, grad_ref,
                 even0, odd0, even1, odd1, products):
    blocks = counts_ref.shape[0]
    rows = pairs_ref.shape[0] // blocks
    even0[...] = start_ref[...]
    odd0[...] = jnp.zeros_like(odd0)
    even1[...] = jnp.zeros_like(even1)
    odd1[...] = jnp.zeros_like(odd1)
    products[...] = jnp.zeros_like(products)

    def steps_of(block):
        return lax.div(counts_ref[block] + (2 * ROWS_STEP - 1), 2 * ROWS_STEP)

    def scatter_block(block, carry):
        def step(at, carry):
            base = pl.multiple_of(block * rows + at * ROWS_STEP, ROWS_STEP)
            scal = block * (2 * rows) + at * ROWS_STEP
            tile = pairs_ref[pl.ds(base, ROWS_STEP), :]
            for r in range(ROWS_STEP):
                row = tile[r:r + 1, :]
                even, odd = (even0, odd0) if r % 2 == 0 else (even1, odd1)
                va = voxel_ref[scal + r]
                vb = voxel_ref[scal + rows + r]
                even[pl.ds(va, 1), :] = even[pl.ds(va, 1), :] + x_ref[scal + r] * row
                odd[pl.ds(vb, 1), :] = odd[pl.ds(vb, 1), :] + x_ref[scal + rows + r] * row
            return carry

        return lax.fori_loop(0, steps_of(block), step, carry)

    lax.fori_loop(0, blocks, scatter_block, 0)

    left = lax.broadcasted_iota(jnp.int32, (LANES, 2 * dirs), 1) < dirs

    def combine(at, carry):
        part = pl.ds(pl.multiple_of(at * LANES, LANES), LANES)
        both = jnp.where(left, even0[part, :] + even1[part, :], odd0[part, :] + odd1[part, :])
        resid_ref[part, :] = both + pltpu.roll(both, dirs, 1)
        return carry

    lax.fori_loop(0, resid_ref.shape[0] // LANES, combine, 0)

    left_row = lax.broadcasted_iota(jnp.int32, (1, 2 * dirs), 1) < dirs

    def gather_block(block, carry):
        def step(at, carry):
            base = pl.multiple_of(block * rows + at * ROWS_STEP, ROWS_STEP)
            scal = block * (2 * rows) + at * ROWS_STEP
            picked = []
            for r in range(ROWS_STEP):
                va = voxel_ref[scal + r]
                vb = voxel_ref[scal + rows + r]
                picked.append(
                    jnp.where(left_row, resid_ref[pl.ds(va, 1), :], resid_ref[pl.ds(vb, 1), :])
                )
            tile = jnp.concatenate(picked, axis=0)
            products[pl.ds(base, ROWS_STEP), :] = tile * pairs_ref[pl.ds(base, ROWS_STEP), :]
            return carry

        return lax.fori_loop(0, steps_of(block), step, carry)

    lax.fori_loop(0, blocks, gather_block, 0)

    half = lax.broadcasted_iota(jnp.int32, (8, 2 * dirs), 0)
    lane = lax.broadcasted_iota(jnp.int32, (8, 2 * dirs), 1)
    select = jnp.where(lax.div(lane, dirs) == half, 1.0, 0.0).astype(jnp.float32)

    def reduce_rows(block, carry):
        part = products[pl.ds(pl.multiple_of(block * rows, rows), rows), :]
        sums = lax.dot_general(
            select, part, (((1,), (1,)), ((), ())), precision=HIGH,
            preferred_element_type=jnp.float32,
        )
        grad_ref[block] = sums[0:2, :]
        return carry

    lax.fori_loop(0, blocks, reduce_rows, 0)


def local_step(voxel, x_slots, counts, pairs, start, dirs):
    blocks = counts.shape[0]
    rows = pairs.shape[0] // blocks
    voxels = start.shape[0]
    vmem = pl.BlockSpec(memory_space=pltpu.VMEM)
    smem = pl.BlockSpec(memory_space=pltpu.SMEM)
    wide = pltpu.VMEM((voxels, 2 * dirs), jnp.float32)
    return pl.pallas_call(
        functools.partial(local_kernel, dirs),
        out_shape=(
            jax.ShapeDtypeStruct((voxels, 2 * dirs), jnp.float32),
            jax.ShapeDtypeStruct((blocks, 2, rows), jnp.float32),
        ),
        in_specs=[smem, smem, smem, vmem, vmem],
        out_specs=(vmem, vmem),
        scratch_shapes=[wide, wide, wide, wide, pltpu.VMEM(pairs.shape, jnp.float32)],
        compiler_params=pltpu.CompilerParams(vmem_limit_bytes=56 * 1024 * 1024),
        cost_estimate=pl.CostEstimate(flops=10**8, bytes_accessed=10**8, transcendentals=0),
    )(voxel, x_slots, counts, pairs, start)


def on_device(shells, weights, seg_streamline, seg_features, pair_counts, seg_voxel, dictionary,
              measured):
    blocks = seg_streamline.shape[2]
    slots = seg_streamline.shape[3]
    coeffs = seg_features.shape[4]
    rows = slots // 2
    dirs = dictionary.shape[1]
    streams = weights.shape[0]
    counts = pair_counts.reshape(blocks)

    owner = seg_streamline.reshape(blocks, rows, 2).transpose(0, 2, 1).reshape(-1)
    voxel = seg_voxel.reshape(blocks, rows, 2).transpose(0, 2, 1).reshape(blocks, slots)
    voxel_all = (
        lax.all_gather(voxel, "shell", axis=0).transpose(1, 0, 2).reshape(blocks * shells * slots)
    )
    dict_all = lax.all_gather(dictionary, "shell", axis=0)

    live = lax.broadcasted_iota(jnp.int32, (blocks, slots), 1) < counts[:, None]
    masked = jnp.where(
        live[:, :, None], seg_features.reshape(blocks, slots, coeffs), jnp.float32(0.0)
    )
    feat_pairs = masked.reshape(blocks * rows, 2 * coeffs)
    sq = jnp.sum((masked * masked).reshape(blocks, rows, 2, coeffs), axis=3)
    sq = sq.transpose(0, 2, 1).reshape(-1)

    hi = (owner // LANES)[:, None] == lax.broadcasted_iota(jnp.int32, (1, streams // LANES), 1)
    lo = (owner % LANES)[:, None] == lax.broadcasted_iota(jnp.int32, (1, LANES), 1)
    hi = hi.astype(jnp.float32)

    def pick(table):
        wide = jnp.dot(hi, table, precision=HIGH)
        return jnp.sum(jnp.where(lo, wide, 0.0), axis=1)

    def add_up(values):
        return lax.dot_general(
            hi, jnp.where(lo, values[:, None], 0.0), (((0,), (0,)), ((), ())), precision=HIGH
        )

    scaling = 0.5 / (0.5 + add_up(sq))

    zero = jnp.zeros_like(dict_all)
    weave = jnp.stack(
        [jnp.concatenate([dict_all, zero], axis=2), jnp.concatenate([zero, dict_all], axis=2)],
        axis=1,
    ).reshape(shells, 2 * coeffs, 2 * dirs)
    projected = jnp.einsum("rk,qkc->qrc", feat_pairs, weave, precision=HIGH)
    projected = projected.reshape(shells, blocks, rows, 2 * dirs).transpose(1, 0, 2, 3)
    pairs = lax.all_to_all(
        projected.reshape(blocks * shells, rows, 2 * dirs), ("space", "shell"), 0, 0, tiled=True
    ).reshape(blocks * shells * rows, 2 * dirs)

    start = jnp.concatenate([-measured.T, jnp.zeros_like(measured).T], axis=1)

    current = weights.reshape(streams // LANES, LANES)
    counts_all = None
    for iteration in range(ITERS):
        sent = pick(current).reshape(blocks, slots)
        if iteration == 0:
            extra = jnp.broadcast_to(counts[:, None].astype(jnp.float32), (blocks, LANES))
            sent = jnp.concatenate([sent, extra], axis=1)
        sent = jnp.broadcast_to(sent[:, None, :], (blocks, shells, sent.shape[1]))
        got = lax.all_to_all(
            sent.reshape(blocks * shells, -1), ("space", "shell"), 0, 0, tiled=True
        )
        if iteration == 0:
            counts_all = got[:, slots].astype(jnp.int32)
        resid, grads = local_step(
            voxel_all, got[:, :slots].reshape(-1), counts_all, pairs, start, dirs
        )
        back = lax.all_to_all(
            grads.reshape(blocks * shells, slots), ("space", "shell"), 0, 0, tiled=True
        )
        slot_grad = jnp.sum(back.reshape(blocks, shells, slots), axis=1)
        current = jnp.maximum(current - scaling * add_up(slot_grad.reshape(-1)), 0.0)
    return current.reshape(streams), resid[:, :dirs].T


def solution(mesh):
    in_specs = (
        P(("space", "shell")),
        P("space", "shell", None, None),
        P("space", "shell", None, None, None),
        P("space", "shell", None),
        P("space", "shell", None, None),
        P(None, "shell"),
        P("shell", "space"),
    )
    out_specs = (P(("space", "shell")), P("shell", "space"))
    return jax.shard_map(
        functools.partial(on_device, mesh.shape["shell"]),
        mesh=mesh, in_specs=in_specs, out_specs=out_specs, check_vma=False,
    )
```

```python
import functools

import jax
import jax.numpy as jnp
from jax import lax
from jax.experimental import pallas as pl
from jax.experimental.pallas import tpu as pltpu
from jax.sharding import PartitionSpec as P

ITERS = 2
LANES = 128
ROWS_STEP = 8
EXTRA = 8
MESH = pl.DeviceIdType.MESH
HIGH = lax.Precision.HIGHEST


def local_kernel(dirs, voxel_ref, x_ref, counts_ref, pairs_ref, start_ref, resid_ref, grad_ref,
                 even0, odd0, even1, odd1, products):
    blocks = counts_ref.shape[0]
    rows = pairs_ref.shape[1] - EXTRA
    even0[...] = start_ref[...]
    odd0[...] = jnp.zeros_like(odd0)
    even1[...] = jnp.zeros_like(even1)
    odd1[...] = jnp.zeros_like(odd1)
    products[...] = jnp.zeros_like(products)

    def steps_of(block):
        return lax.div(counts_ref[block] + (2 * ROWS_STEP - 1), 2 * ROWS_STEP)

    def scatter_block(block, carry):
        def step(at, carry):
            scal = block * (2 * rows) + at * ROWS_STEP
            tile = pairs_ref[block, pl.ds(pl.multiple_of(at * ROWS_STEP, ROWS_STEP), ROWS_STEP), :]
            for r in range(ROWS_STEP):
                row = tile[r:r + 1, :]
                even, odd = (even0, odd0) if r % 2 == 0 else (even1, odd1)
                va = voxel_ref[scal + r]
                vb = voxel_ref[scal + rows + r]
                even[pl.ds(va, 1), :] = even[pl.ds(va, 1), :] + x_ref[scal + r] * row
                odd[pl.ds(vb, 1), :] = odd[pl.ds(vb, 1), :] + x_ref[scal + rows + r] * row
            return carry

        return lax.fori_loop(0, steps_of(block), step, carry)

    lax.fori_loop(0, blocks, scatter_block, 0)

    left = lax.broadcasted_iota(jnp.int32, (LANES, 2 * dirs), 1) < dirs

    def combine(at, carry):
        part = pl.ds(pl.multiple_of(at * LANES, LANES), LANES)
        both = jnp.where(left, even0[part, :] + even1[part, :], odd0[part, :] + odd1[part, :])
        resid_ref[part, :] = both + pltpu.roll(both, dirs, 1)
        return carry

    lax.fori_loop(0, resid_ref.shape[0] // LANES, combine, 0)

    left_row = lax.broadcasted_iota(jnp.int32, (1, 2 * dirs), 1) < dirs

    def gather_block(block, carry):
        def step(at, carry):
            base = pl.multiple_of(block * rows + at * ROWS_STEP, ROWS_STEP)
            scal = block * (2 * rows) + at * ROWS_STEP
            picked = []
            for r in range(ROWS_STEP):
                va = voxel_ref[scal + r]
                vb = voxel_ref[scal + rows + r]
                picked.append(
                    jnp.where(left_row, resid_ref[pl.ds(va, 1), :], resid_ref[pl.ds(vb, 1), :])
                )
            tile = jnp.concatenate(picked, axis=0)
            part = pl.ds(pl.multiple_of(at * ROWS_STEP, ROWS_STEP), ROWS_STEP)
            products[pl.ds(base, ROWS_STEP), :] = tile * pairs_ref[block, part, :]
            return carry

        return lax.fori_loop(0, steps_of(block), step, carry)

    lax.fori_loop(0, blocks, gather_block, 0)

    half = lax.broadcasted_iota(jnp.int32, (8, 2 * dirs), 0)
    lane = lax.broadcasted_iota(jnp.int32, (8, 2 * dirs), 1)
    select = jnp.where(lax.div(lane, dirs) == half, 1.0, 0.0).astype(jnp.float32)

    def reduce_rows(block, carry):
        part = products[pl.ds(pl.multiple_of(block * rows, rows), rows), :]
        sums = lax.dot_general(
            select, part, (((1,), (1,)), ((), ())), precision=HIGH,
            preferred_element_type=jnp.float32,
        )
        grad_ref[block] = sums
        return carry

    lax.fori_loop(0, blocks, reduce_rows, 0)


def local_step(voxel, x_slots, counts, pairs, start, dirs):
    blocks = counts.shape[0]
    rows = pairs.shape[1] - EXTRA
    voxels = start.shape[0]
    vmem = pl.BlockSpec(memory_space=pltpu.VMEM)
    smem = pl.BlockSpec(memory_space=pltpu.SMEM)
    wide = pltpu.VMEM((voxels, 2 * dirs), jnp.float32)
    return pl.pallas_call(
        functools.partial(local_kernel, dirs),
        out_shape=(
            jax.ShapeDtypeStruct((voxels, 2 * dirs), jnp.float32),
            jax.ShapeDtypeStruct((blocks, 8, rows), jnp.float32),
        ),
        in_specs=[smem, smem, smem, vmem, vmem],
        out_specs=(vmem, vmem),
        scratch_shapes=[wide, wide, wide, wide, pltpu.VMEM((blocks * rows, 2 * dirs), jnp.float32)],
        compiler_params=pltpu.CompilerParams(vmem_limit_bytes=56 * 1024 * 1024),
        cost_estimate=pl.CostEstimate(flops=10**8, bytes_accessed=10**8, transcendentals=0),
    )(voxel, x_slots, counts, pairs, start)


def greet_all(spaces, shells, me_space, me_shell):
    total = spaces * shells
    me = me_space * shells + me_shell
    barrier = pltpu.get_barrier_semaphore()

    def greet(k, carry):
        other = lax.rem(me + k, total)
        pl.semaphore_signal(
            barrier, inc=1, device_id=(lax.div(other, shells), lax.rem(other, shells)),
            device_id_type=MESH,
        )
        return carry

    lax.fori_loop(1, total, greet, 0)
    pl.semaphore_wait(barrier, total - 1)


def exchange_kernel(spaces, shells, feat_ref, head_ref, small_ref, pairs_ref, heads_ref,
                    sent, woven, send_sem, recv_sem, head_send, head_recv):
    me_space, me_shell = lax.axis_index("space"), lax.axis_index("shell")
    me = me_space * shells + me_shell
    total = spaces * shells
    rows = feat_ref.shape[0] // spaces
    coeffs = feat_ref.shape[1] // 2
    dirs = sent.shape[2] // 2
    greet_all(spaces, shells, me_space, me_shell)

    heads_ref[me_shell] = head_ref[...]

    def head_copy(k):
        other = lax.rem(me_shell + k, shells)
        return pltpu.make_async_remote_copy(
            src_ref=head_ref, dst_ref=heads_ref.at[me_shell],
            send_sem=head_send.at[k], recv_sem=head_recv.at[k],
            device_id=(me_space, other), device_id_type=MESH,
        )

    for k in range(1, shells):
        head_copy(k).start()

    def copy_to(space, shell):
        at = space * shells + shell
        return pltpu.make_async_remote_copy(
            src_ref=sent.at[at], dst_ref=pairs_ref.at[me],
            send_sem=send_sem.at[at], recv_sem=recv_sem.at[me],
            device_id=(space, shell), device_id_type=MESH,
        )

    woven[...] = jnp.zeros_like(woven)
    for k in range(shells):
        shell = lax.rem(me_shell + shells - k, shells)
        if k > 0:
            head_copy(k).wait_recv()
        part = heads_ref[shell, 0:dirs, :]
        woven[0:dirs, 0:coeffs] = part
        woven[dirs:2 * dirs, coeffs:2 * coeffs] = part

        def send(step, carry):
            space = lax.rem(me_space + step, spaces)
            block = feat_ref[pl.ds(pl.multiple_of(space * rows, rows), rows), :]
            value = lax.dot_general(
                block, woven[...], (((1,), (1,)), ((), ())), precision=HIGH,
                preferred_element_type=jnp.float32,
            )
            at = space * shells + shell
            sent[at, 0:rows, :] = value
            sent[at, rows:rows + EXTRA, :] = small_ref[space]
            copy_to(space, shell).start()
            return carry

        if k == 0:
            value = lax.dot_general(
                feat_ref[pl.ds(pl.multiple_of(me_space * rows, rows), rows), :], woven[...],
                (((1,), (1,)), ((), ())), precision=HIGH, preferred_element_type=jnp.float32,
            )
            pairs_ref[me, 0:rows, :] = value
            pairs_ref[me, rows:rows + EXTRA, :] = small_ref[me_space]
        lax.fori_loop(1 if k == 0 else 0, spaces, send, 0)

    def finish(k, carry):
        other = lax.rem(me + k, total)
        space, shell = lax.div(other, shells), lax.rem(other, shells)
        copy_to(space, shell).wait_send()
        pltpu.make_async_remote_copy(
            src_ref=sent.at[other], dst_ref=pairs_ref.at[other],
            send_sem=send_sem.at[other], recv_sem=recv_sem.at[other],
            device_id=(space, shell), device_id_type=MESH,
        ).wait_recv()
        return carry

    lax.fori_loop(1, total, finish, 0)
    for k in range(1, shells):
        head_copy(k).wait_send()


def exchange(spaces, shells, feat_pairs, head, small):
    rows = feat_pairs.shape[0] // spaces
    dirs = head.shape[0] - 2 * spaces
    total = spaces * shells
    vmem = pl.BlockSpec(memory_space=pltpu.VMEM)
    out = (total, rows + EXTRA, 2 * dirs)
    return pl.pallas_call(
        functools.partial(exchange_kernel, spaces, shells),
        out_shape=(
            jax.ShapeDtypeStruct(out, jnp.float32),
            jax.ShapeDtypeStruct((shells,) + head.shape, jnp.float32),
        ),
        in_specs=[vmem] * 3,
        out_specs=(vmem, vmem),
        scratch_shapes=[
            pltpu.VMEM(out, jnp.float32),
            pltpu.VMEM((2 * dirs, feat_pairs.shape[1]), jnp.float32),
            pltpu.SemaphoreType.DMA((total,)),
            pltpu.SemaphoreType.DMA((total,)),
            pltpu.SemaphoreType.DMA((shells,)),
            pltpu.SemaphoreType.DMA((shells,)),
        ],
        compiler_params=pltpu.CompilerParams(
            collective_id=0, has_side_effects=True, vmem_limit_bytes=56 * 1024 * 1024
        ),
    )(feat_pairs, head, small)


def message_kernel(spaces, shells, shared, from_ref, to_ref, send_sem, recv_sem):
    me_space, me_shell = lax.axis_index("space"), lax.axis_index("shell")
    me = me_space * shells + me_shell
    total = spaces * shells
    greet_all(spaces, shells, me_space, me_shell)

    def source(at):
        return lax.div(at, shells) if shared else at

    def copy_of(other, slot):
        return pltpu.make_async_remote_copy(
            src_ref=from_ref.at[source(other)], dst_ref=to_ref.at[slot],
            send_sem=send_sem.at[other], recv_sem=recv_sem.at[slot],
            device_id=(lax.div(other, shells), lax.rem(other, shells)), device_id_type=MESH,
        )

    def send(k, carry):
        copy_of(lax.rem(me + k, total), me).start()
        return carry

    lax.fori_loop(1, total, send, 0)
    to_ref[me] = from_ref[source(me)]

    def finish(k, carry):
        other = lax.rem(me + k, total)
        copy_of(other, me).wait_send()
        copy_of(other, other).wait_recv()
        return carry

    lax.fori_loop(1, total, finish, 0)


def message(spaces, shells, shared, values):
    total = spaces * shells
    vmem = pl.BlockSpec(memory_space=pltpu.VMEM)
    return pl.pallas_call(
        functools.partial(message_kernel, spaces, shells, shared),
        out_shape=jax.ShapeDtypeStruct((total,) + values.shape[1:], jnp.float32),
        in_specs=[vmem],
        out_specs=vmem,
        scratch_shapes=[pltpu.SemaphoreType.DMA((total,)), pltpu.SemaphoreType.DMA((total,))],
        compiler_params=pltpu.CompilerParams(
            collective_id=2 if shared else 1, has_side_effects=True
        ),
    )(values)


def on_device(spaces, shells, weights, seg_streamline, seg_features, pair_counts, seg_voxel, dictionary,
              measured):
    blocks = seg_streamline.shape[2]
    slots = seg_streamline.shape[3]
    coeffs = seg_features.shape[4]
    rows = slots // 2
    dirs = dictionary.shape[1]
    streams = weights.shape[0]
    counts = pair_counts.reshape(blocks)

    owner = seg_streamline.reshape(blocks, rows, 2).transpose(0, 2, 1).reshape(-1)
    voxel = seg_voxel.reshape(blocks, rows, 2).transpose(0, 2, 1).reshape(blocks, slots)
    head = jnp.concatenate(
        [dictionary.T, voxel.reshape(2 * blocks, rows).astype(jnp.float32)], axis=0
    )

    live = lax.broadcasted_iota(jnp.int32, (blocks, slots), 1) < counts[:, None]
    masked = jnp.where(
        live[:, :, None], seg_features.reshape(blocks, slots, coeffs), jnp.float32(0.0)
    )
    feat_pairs = masked.reshape(blocks * rows, 2 * coeffs)
    sq = jnp.sum((masked * masked).reshape(blocks, rows, 2, coeffs), axis=3)
    sq = sq.transpose(0, 2, 1).reshape(-1)

    hi = (owner // LANES)[:, None] == lax.broadcasted_iota(jnp.int32, (1, streams // LANES), 1)
    lo = (owner % LANES)[:, None] == lax.broadcasted_iota(jnp.int32, (1, LANES), 1)
    hi = hi.astype(jnp.float32)

    def pick(table):
        wide = jnp.dot(hi, table, precision=HIGH)
        return jnp.sum(jnp.where(lo, wide, 0.0), axis=1)

    def add_up(values):
        return lax.dot_general(
            hi, jnp.where(lo, values[:, None], 0.0), (((0,), (0,)), ((), ())), precision=HIGH
        )

    scaling = 0.5 / (0.5 + add_up(sq))

    current = weights.reshape(streams // LANES, LANES)
    extra = jnp.broadcast_to(counts[:, None, None].astype(jnp.float32), (blocks, EXTRA - 2, rows))
    small = jnp.concatenate([pick(current).reshape(blocks, 2, rows), extra], axis=1)
    pairs, heads = exchange(spaces, shells, feat_pairs, head, small)
    voxel_all = heads[:, dirs:, :].astype(jnp.int32).reshape(shells, blocks, slots)
    voxel_all = voxel_all.transpose(1, 0, 2).reshape(-1)
    x_slots = pairs[:, rows:rows + 2, :].reshape(-1)
    counts_all = pairs[:, rows + 2, 0].astype(jnp.int32)

    start = jnp.concatenate([-measured.T, jnp.zeros_like(measured).T], axis=1)

    for iteration in range(ITERS):
        resid, grads = local_step(voxel_all, x_slots, counts_all, pairs, start, dirs)
        back = message(spaces, shells, False, grads)
        slot_grad = jnp.sum(back.reshape(blocks, shells, 8, rows)[:, :, 0:2], axis=1)
        current = jnp.maximum(current - scaling * add_up(slot_grad.reshape(-1)), 0.0)
        if iteration < ITERS - 1:
            sent = jnp.pad(pick(current).reshape(blocks, 2, rows), ((0, 0), (0, 6), (0, 0)))
            x_slots = message(spaces, shells, True, sent)[:, 0:2, :].reshape(-1)
    return current.reshape(streams), resid[:, :dirs].T


def solution(mesh):
    in_specs = (
        P(("space", "shell")),
        P("space", "shell", None, None),
        P("space", "shell", None, None, None),
        P("space", "shell", None),
        P("space", "shell", None, None),
        P(None, "shell"),
        P("shell", "space"),
    )
    out_specs = (P(("space", "shell")), P("shell", "space"))
    return jax.shard_map(
        functools.partial(on_device, mesh.shape["space"], mesh.shape["shell"]),
        mesh=mesh, in_specs=in_specs, out_specs=out_specs, check_vma=False,
    )
```

```python
import functools

import jax
import jax.numpy as jnp
from jax import lax
from jax.experimental import pallas as pl
from jax.experimental.pallas import tpu as pltpu
from jax.sharding import PartitionSpec as P

ITERS = 2
LANES = 128
ROWS_STEP = 8
EXTRA = 8
MESH = pl.DeviceIdType.MESH
HIGH = lax.Precision.HIGHEST


def local_kernel(dirs, voxel_ref, x_ref, counts_ref, pairs_ref, start_ref, resid_ref, grad_ref,
                 even0, odd0, even1, odd1, products):
    blocks = counts_ref.shape[0]
    rows = pairs_ref.shape[1] - EXTRA
    even0[...] = start_ref[...]
    odd0[...] = jnp.zeros_like(odd0)
    even1[...] = jnp.zeros_like(even1)
    odd1[...] = jnp.zeros_like(odd1)
    products[...] = jnp.zeros_like(products)

    def steps_of(block):
        return lax.div(counts_ref[block] + (2 * ROWS_STEP - 1), 2 * ROWS_STEP)

    def scatter_block(block, carry):
        def step(at, carry):
            scal = block * (2 * rows) + at * ROWS_STEP
            tile = pairs_ref[block, pl.ds(pl.multiple_of(at * ROWS_STEP, ROWS_STEP), ROWS_STEP), :]
            for r in range(ROWS_STEP):
                row = tile[r:r + 1, :]
                even, odd = (even0, odd0) if r % 2 == 0 else (even1, odd1)
                va = voxel_ref[scal + r]
                vb = voxel_ref[scal + rows + r]
                even[pl.ds(va, 1), :] = even[pl.ds(va, 1), :] + x_ref[block, 0, at * ROWS_STEP + r] * row
                odd[pl.ds(vb, 1), :] = odd[pl.ds(vb, 1), :] + x_ref[block, 1, at * ROWS_STEP + r] * row
            return carry

        return lax.fori_loop(0, steps_of(block), step, carry)

    lax.fori_loop(0, blocks, scatter_block, 0)

    left = lax.broadcasted_iota(jnp.int32, (LANES, 2 * dirs), 1) < dirs

    def combine(at, carry):
        part = pl.ds(pl.multiple_of(at * LANES, LANES), LANES)
        both = jnp.where(left, even0[part, :] + even1[part, :], odd0[part, :] + odd1[part, :])
        resid_ref[part, :] = both + pltpu.roll(both, dirs, 1)
        return carry

    lax.fori_loop(0, resid_ref.shape[0] // LANES, combine, 0)

    left_row = lax.broadcasted_iota(jnp.int32, (1, 2 * dirs), 1) < dirs

    def gather_block(block, carry):
        def step(at, carry):
            base = pl.multiple_of(block * rows + at * ROWS_STEP, ROWS_STEP)
            scal = block * (2 * rows) + at * ROWS_STEP
            picked = []
            for r in range(ROWS_STEP):
                va = voxel_ref[scal + r]
                vb = voxel_ref[scal + rows + r]
                picked.append(
                    jnp.where(left_row, resid_ref[pl.ds(va, 1), :], resid_ref[pl.ds(vb, 1), :])
                )
            tile = jnp.concatenate(picked, axis=0)
            part = pl.ds(pl.multiple_of(at * ROWS_STEP, ROWS_STEP), ROWS_STEP)
            products[pl.ds(base, ROWS_STEP), :] = tile * pairs_ref[block, part, :]
            return carry

        return lax.fori_loop(0, steps_of(block), step, carry)

    lax.fori_loop(0, blocks, gather_block, 0)

    half = lax.broadcasted_iota(jnp.int32, (8, 2 * dirs), 0)
    lane = lax.broadcasted_iota(jnp.int32, (8, 2 * dirs), 1)
    select = jnp.where(lax.div(lane, dirs) == half, 1.0, 0.0).astype(jnp.float32)

    def reduce_rows(block, carry):
        part = products[pl.ds(pl.multiple_of(block * rows, rows), rows), :]
        sums = lax.dot_general(
            select, part, (((1,), (1,)), ((), ())), precision=HIGH,
            preferred_element_type=jnp.float32,
        )
        grad_ref[block] = sums[0:2, :]
        return carry

    lax.fori_loop(0, blocks, reduce_rows, 0)


def local_step(voxel, x_slots, counts, pairs, start, dirs):
    blocks = counts.shape[0]
    rows = pairs.shape[1] - EXTRA
    voxels = start.shape[0]
    vmem = pl.BlockSpec(memory_space=pltpu.VMEM)
    smem = pl.BlockSpec(memory_space=pltpu.SMEM)
    wide = pltpu.VMEM((voxels, 2 * dirs), jnp.float32)
    return pl.pallas_call(
        functools.partial(local_kernel, dirs),
        out_shape=(
            jax.ShapeDtypeStruct((voxels, 2 * dirs), jnp.float32),
            jax.ShapeDtypeStruct((blocks, 2, rows), jnp.float32),
        ),
        in_specs=[smem, smem, smem, vmem, vmem],
        out_specs=(vmem, vmem),
        scratch_shapes=[wide, wide, wide, wide, pltpu.VMEM((blocks * rows, 2 * dirs), jnp.float32)],
        compiler_params=pltpu.CompilerParams(vmem_limit_bytes=56 * 1024 * 1024),
        cost_estimate=pl.CostEstimate(flops=10**8, bytes_accessed=10**8, transcendentals=0),
    )(voxel, x_slots, counts, pairs, start)


def greet_all(spaces, shells, me_space, me_shell):
    total = spaces * shells
    me = me_space * shells + me_shell
    barrier = pltpu.get_barrier_semaphore()

    def greet(k, carry):
        other = lax.rem(me + k, total)
        pl.semaphore_signal(
            barrier, inc=1, device_id=(lax.div(other, shells), lax.rem(other, shells)),
            device_id_type=MESH,
        )
        return carry

    lax.fori_loop(1, total, greet, 0)
    pl.semaphore_wait(barrier, total - 1)


def exchange_kernel(spaces, shells, feat_ref, head_ref, small_ref, pairs_ref, heads_ref,
                    sent, woven, send_sem, recv_sem, head_send, head_recv):
    me_space, me_shell = lax.axis_index("space"), lax.axis_index("shell")
    me = me_space * shells + me_shell
    total = spaces * shells
    rows = feat_ref.shape[0] // spaces
    coeffs = feat_ref.shape[1] // 2
    dirs = sent.shape[2] // 2
    greet_all(spaces, shells, me_space, me_shell)

    heads_ref[me_shell] = head_ref[...]

    def head_copy(k):
        other = lax.rem(me_shell + k, shells)
        return pltpu.make_async_remote_copy(
            src_ref=head_ref, dst_ref=heads_ref.at[me_shell],
            send_sem=head_send.at[k], recv_sem=head_recv.at[k],
            device_id=(me_space, other), device_id_type=MESH,
        )

    for k in range(1, shells):
        head_copy(k).start()

    def copy_to(space, shell):
        at = space * shells + shell
        return pltpu.make_async_remote_copy(
            src_ref=sent.at[at], dst_ref=pairs_ref.at[me],
            send_sem=send_sem.at[at], recv_sem=recv_sem.at[me],
            device_id=(space, shell), device_id_type=MESH,
        )

    woven[...] = jnp.zeros_like(woven)
    for k in range(shells):
        shell = lax.rem(me_shell + shells - k, shells)
        if k > 0:
            head_copy(k).wait_recv()
        part = heads_ref[shell, 0:dirs, :]
        woven[0:dirs, 0:coeffs] = part
        woven[dirs:2 * dirs, coeffs:2 * coeffs] = part

        def send(step, carry):
            space = lax.rem(me_space + step, spaces)
            block = feat_ref[pl.ds(pl.multiple_of(space * rows, rows), rows), :]
            value = lax.dot_general(
                block, woven[...], (((1,), (1,)), ((), ())), precision=HIGH,
                preferred_element_type=jnp.float32,
            )
            at = space * shells + shell
            sent[at, 0:rows, :] = value
            sent[at, rows:rows + EXTRA, :] = small_ref[space]
            copy_to(space, shell).start()
            return carry

        if k == 0:
            value = lax.dot_general(
                feat_ref[pl.ds(pl.multiple_of(me_space * rows, rows), rows), :], woven[...],
                (((1,), (1,)), ((), ())), precision=HIGH, preferred_element_type=jnp.float32,
            )
            pairs_ref[me, 0:rows, :] = value
            pairs_ref[me, rows:rows + EXTRA, :] = small_ref[me_space]
        lax.fori_loop(1 if k == 0 else 0, spaces, send, 0)

    def finish(k, carry):
        other = lax.rem(me + k, total)
        space, shell = lax.div(other, shells), lax.rem(other, shells)
        copy_to(space, shell).wait_send()
        pltpu.make_async_remote_copy(
            src_ref=sent.at[other], dst_ref=pairs_ref.at[other],
            send_sem=send_sem.at[other], recv_sem=recv_sem.at[other],
            device_id=(space, shell), device_id_type=MESH,
        ).wait_recv()
        return carry

    lax.fori_loop(1, total, finish, 0)
    for k in range(1, shells):
        head_copy(k).wait_send()


def exchange(spaces, shells, feat_pairs, head, small):
    rows = feat_pairs.shape[0] // spaces
    dirs = head.shape[0] - 2 * spaces
    total = spaces * shells
    vmem = pl.BlockSpec(memory_space=pltpu.VMEM)
    out = (total, rows + EXTRA, 2 * dirs)
    return pl.pallas_call(
        functools.partial(exchange_kernel, spaces, shells),
        out_shape=(
            jax.ShapeDtypeStruct(out, jnp.float32),
            jax.ShapeDtypeStruct((shells,) + head.shape, jnp.float32),
        ),
        in_specs=[vmem] * 3,
        out_specs=(vmem, vmem),
        scratch_shapes=[
            pltpu.VMEM(out, jnp.float32),
            pltpu.VMEM((2 * dirs, feat_pairs.shape[1]), jnp.float32),
            pltpu.SemaphoreType.DMA((total,)),
            pltpu.SemaphoreType.DMA((total,)),
            pltpu.SemaphoreType.DMA((shells,)),
            pltpu.SemaphoreType.DMA((shells,)),
        ],
        compiler_params=pltpu.CompilerParams(
            collective_id=0, has_side_effects=True, vmem_limit_bytes=56 * 1024 * 1024
        ),
    )(feat_pairs, head, small)


def message_kernel(spaces, shells, shared, from_ref, to_ref, send_sem, recv_sem):
    me_space, me_shell = lax.axis_index("space"), lax.axis_index("shell")
    me = me_space * shells + me_shell
    total = spaces * shells
    greet_all(spaces, shells, me_space, me_shell)

    def source(at):
        return lax.div(at, shells) if shared else at

    def copy_of(other, slot):
        return pltpu.make_async_remote_copy(
            src_ref=from_ref.at[source(other)], dst_ref=to_ref.at[slot],
            send_sem=send_sem.at[other], recv_sem=recv_sem.at[slot],
            device_id=(lax.div(other, shells), lax.rem(other, shells)), device_id_type=MESH,
        )

    def send(k, carry):
        copy_of(lax.rem(me + k, total), me).start()
        return carry

    lax.fori_loop(1, total, send, 0)
    to_ref[me] = from_ref[source(me)]

    def finish(k, carry):
        other = lax.rem(me + k, total)
        copy_of(other, me).wait_send()
        copy_of(other, other).wait_recv()
        return carry

    lax.fori_loop(1, total, finish, 0)


def message(spaces, shells, shared, values):
    total = spaces * shells
    vmem = pl.BlockSpec(memory_space=pltpu.VMEM)
    return pl.pallas_call(
        functools.partial(message_kernel, spaces, shells, shared),
        out_shape=jax.ShapeDtypeStruct((total,) + values.shape[1:], jnp.float32),
        in_specs=[vmem],
        out_specs=vmem,
        scratch_shapes=[pltpu.SemaphoreType.DMA((total,)), pltpu.SemaphoreType.DMA((total,))],
        compiler_params=pltpu.CompilerParams(
            collective_id=2 if shared else 1, has_side_effects=True
        ),
    )(values)


def on_device(spaces, shells, weights, seg_streamline, seg_features, pair_counts, seg_voxel, dictionary,
              measured):
    blocks = seg_streamline.shape[2]
    slots = seg_streamline.shape[3]
    coeffs = seg_features.shape[4]
    rows = slots // 2
    dirs = dictionary.shape[1]
    streams = weights.shape[0]
    counts = pair_counts.reshape(blocks)

    owner = seg_streamline.reshape(blocks, rows, 2).transpose(0, 2, 1).reshape(-1)
    voxel = seg_voxel.reshape(blocks, rows, 2).transpose(0, 2, 1).reshape(blocks, slots)
    head = jnp.concatenate(
        [dictionary.T, voxel.reshape(2 * blocks, rows).astype(jnp.float32)], axis=0
    )

    live = lax.broadcasted_iota(jnp.int32, (blocks, slots), 1) < counts[:, None]
    masked = jnp.where(
        live[:, :, None], seg_features.reshape(blocks, slots, coeffs), jnp.float32(0.0)
    )
    feat_pairs = masked.reshape(blocks * rows, 2 * coeffs)
    sq = jnp.sum((masked * masked).reshape(blocks, rows, 2, coeffs), axis=3)
    sq = sq.transpose(0, 2, 1).reshape(-1)

    hi = (owner // LANES)[:, None] == lax.broadcasted_iota(jnp.int32, (1, streams // LANES), 1)
    lo = (owner % LANES)[:, None] == lax.broadcasted_iota(jnp.int32, (1, LANES), 1)
    hi = hi.astype(jnp.float32)

    def pick(table):
        wide = jnp.dot(hi, table, precision=HIGH)
        return jnp.sum(jnp.where(lo, wide, 0.0), axis=1)

    def add_up(values):
        return lax.dot_general(
            hi, jnp.where(lo, values[:, None], 0.0), (((0,), (0,)), ((), ())), precision=HIGH
        )

    scaling = 0.5 / (0.5 + add_up(sq))

    current = weights.reshape(streams // LANES, LANES)
    extra = jnp.broadcast_to(counts[:, None, None].astype(jnp.float32), (blocks, EXTRA - 2, rows))
    small = jnp.concatenate([pick(current).reshape(blocks, 2, rows), extra], axis=1)
    pairs, heads = exchange(spaces, shells, feat_pairs, head, small)
    voxel_all = heads[:, dirs:, :].astype(jnp.int32).reshape(shells, blocks, slots)
    voxel_all = voxel_all.transpose(1, 0, 2).reshape(-1)
    x_slots = pairs[:, rows:rows + 2, :]
    counts_all = pairs[:, rows + 2, 0].astype(jnp.int32)

    start = jnp.concatenate([-measured.T, jnp.zeros_like(measured).T], axis=1)

    for iteration in range(ITERS):
        resid, grads = local_step(voxel_all, x_slots, counts_all, pairs, start, dirs)
        back = message(spaces, shells, False, grads)
        slot_grad = jnp.sum(back.reshape(blocks, shells, 2, rows), axis=1)
        current = jnp.maximum(current - scaling * add_up(slot_grad.reshape(-1)), 0.0)
        if iteration < ITERS - 1:
            x_slots = message(spaces, shells, True, pick(current).reshape(blocks, 2, rows))
    return current.reshape(streams), resid[:, :dirs].T


def solution(mesh):
    in_specs = (
        P(("space", "shell")),
        P("space", "shell", None, None),
        P("space", "shell", None, None, None),
        P("space", "shell", None),
        P("space", "shell", None, None),
        P(None, "shell"),
        P("shell", "space"),
    )
    out_specs = (P(("space", "shell")), P("shell", "space"))
    return jax.shard_map(
        functools.partial(on_device, mesh.shape["space"], mesh.shape["shell"]),
        mesh=mesh, in_specs=in_specs, out_specs=out_specs, check_vma=False,
    )
```

```python
import functools

import jax
import jax.numpy as jnp
from jax import lax
from jax.experimental import pallas as pl
from jax.experimental.pallas import tpu as pltpu
from jax.sharding import PartitionSpec as P

ITERS = 2
LANES = 128
ROWS_STEP = 8
EXTRA = 8
MESH = pl.DeviceIdType.MESH
HIGH = lax.Precision.HIGHEST


def local_kernel(dirs, voxel_ref, x_ref, counts_ref, pairs_ref, start_ref, resid_ref, grad_ref,
                 even0, odd0, even1, odd1, products):
    blocks = counts_ref.shape[0]
    rows = pairs_ref.shape[1] - EXTRA
    even0[...] = start_ref[...]
    odd0[...] = jnp.zeros_like(odd0)
    even1[...] = jnp.zeros_like(even1)
    odd1[...] = jnp.zeros_like(odd1)
    products[...] = jnp.zeros_like(products)

    def steps_of(block):
        return lax.div(counts_ref[block] + (2 * ROWS_STEP - 1), 2 * ROWS_STEP)

    def scatter_block(block, carry):
        def step(at, carry):
            scal = block * (2 * rows) + at * ROWS_STEP
            tile = pairs_ref[block, pl.ds(pl.multiple_of(at * ROWS_STEP, ROWS_STEP), ROWS_STEP), :]
            for r in range(ROWS_STEP):
                row = tile[r:r + 1, :]
                even, odd = (even0, odd0) if r % 2 == 0 else (even1, odd1)
                va = voxel_ref[scal + r]
                vb = voxel_ref[scal + rows + r]
                even[pl.ds(va, 1), :] = even[pl.ds(va, 1), :] + x_ref[scal + r] * row
                odd[pl.ds(vb, 1), :] = odd[pl.ds(vb, 1), :] + x_ref[scal + rows + r] * row
            return carry

        return lax.fori_loop(0, steps_of(block), step, carry)

    lax.fori_loop(0, blocks, scatter_block, 0)

    left = lax.broadcasted_iota(jnp.int32, (LANES, 2 * dirs), 1) < dirs

    def combine(at, carry):
        part = pl.ds(pl.multiple_of(at * LANES, LANES), LANES)
        both = jnp.where(left, even0[part, :] + even1[part, :], odd0[part, :] + odd1[part, :])
        resid_ref[part, :] = both + pltpu.roll(both, dirs, 1)
        return carry

    lax.fori_loop(0, resid_ref.shape[0] // LANES, combine, 0)

    left_row = lax.broadcasted_iota(jnp.int32, (1, 2 * dirs), 1) < dirs

    def gather_block(block, carry):
        def step(at, carry):
            base = pl.multiple_of(block * rows + at * ROWS_STEP, ROWS_STEP)
            scal = block * (2 * rows) + at * ROWS_STEP
            picked = []
            for r in range(ROWS_STEP):
                va = voxel_ref[scal + r]
                vb = voxel_ref[scal + rows + r]
                picked.append(
                    jnp.where(left_row, resid_ref[pl.ds(va, 1), :], resid_ref[pl.ds(vb, 1), :])
                )
            tile = jnp.concatenate(picked, axis=0)
            part = pl.ds(pl.multiple_of(at * ROWS_STEP, ROWS_STEP), ROWS_STEP)
            products[pl.ds(base, ROWS_STEP), :] = tile * pairs_ref[block, part, :]
            return carry

        return lax.fori_loop(0, steps_of(block), step, carry)

    lax.fori_loop(0, blocks, gather_block, 0)

    half = lax.broadcasted_iota(jnp.int32, (8, 2 * dirs), 0)
    lane = lax.broadcasted_iota(jnp.int32, (8, 2 * dirs), 1)
    select = jnp.where(lax.div(lane, dirs) == half, 1.0, 0.0).astype(jnp.float32)

    def reduce_rows(block, carry):
        part = products[pl.ds(pl.multiple_of(block * rows, rows), rows), :]
        sums = lax.dot_general(
            select, part, (((1,), (1,)), ((), ())), precision=HIGH,
            preferred_element_type=jnp.float32,
        )
        grad_ref[block] = sums[0:2, :]
        return carry

    lax.fori_loop(0, blocks, reduce_rows, 0)


def local_step(voxel, x_slots, counts, pairs, start, dirs):
    blocks = counts.shape[0]
    rows = pairs.shape[1] - EXTRA
    voxels = start.shape[0]
    vmem = pl.BlockSpec(memory_space=pltpu.VMEM)
    smem = pl.BlockSpec(memory_space=pltpu.SMEM)
    wide = pltpu.VMEM((voxels, 2 * dirs), jnp.float32)
    x_slots = x_slots.reshape(-1)
    return pl.pallas_call(
        functools.partial(local_kernel, dirs),
        out_shape=(
            jax.ShapeDtypeStruct((voxels, 2 * dirs), jnp.float32),
            jax.ShapeDtypeStruct((blocks, 2, rows), jnp.float32),
        ),
        in_specs=[smem, smem, smem, vmem, vmem],
        out_specs=(vmem, vmem),
        scratch_shapes=[wide, wide, wide, wide, pltpu.VMEM((blocks * rows, 2 * dirs), jnp.float32)],
        compiler_params=pltpu.CompilerParams(vmem_limit_bytes=56 * 1024 * 1024),
        cost_estimate=pl.CostEstimate(flops=10**8, bytes_accessed=10**8, transcendentals=0),
    )(voxel, x_slots, counts, pairs, start)


def greet_all(spaces, shells, me_space, me_shell):
    total = spaces * shells
    me = me_space * shells + me_shell
    barrier = pltpu.get_barrier_semaphore()

    def greet(k, carry):
        other = lax.rem(me + k, total)
        pl.semaphore_signal(
            barrier, inc=1, device_id=(lax.div(other, shells), lax.rem(other, shells)),
            device_id_type=MESH,
        )
        return carry

    lax.fori_loop(1, total, greet, 0)
    pl.semaphore_wait(barrier, total - 1)


def exchange_kernel(spaces, shells, feat_ref, head_ref, small_ref, pairs_ref, heads_ref,
                    sent, woven, send_sem, recv_sem, head_send, head_recv):
    me_space, me_shell = lax.axis_index("space"), lax.axis_index("shell")
    me = me_space * shells + me_shell
    total = spaces * shells
    rows = feat_ref.shape[0] // spaces
    coeffs = feat_ref.shape[1] // 2
    dirs = sent.shape[2] // 2
    greet_all(spaces, shells, me_space, me_shell)

    heads_ref[me_shell] = head_ref[...]

    def head_copy(k):
        other = lax.rem(me_shell + k, shells)
        return pltpu.make_async_remote_copy(
            src_ref=head_ref, dst_ref=heads_ref.at[me_shell],
            send_sem=head_send.at[k], recv_sem=head_recv.at[k],
            device_id=(me_space, other), device_id_type=MESH,
        )

    for k in range(1, shells):
        head_copy(k).start()

    def copy_to(space, shell):
        at = space * shells + shell
        return pltpu.make_async_remote_copy(
            src_ref=sent.at[at], dst_ref=pairs_ref.at[me],
            send_sem=send_sem.at[at], recv_sem=recv_sem.at[me],
            device_id=(space, shell), device_id_type=MESH,
        )

    woven[...] = jnp.zeros_like(woven)
    for k in range(shells):
        shell = lax.rem(me_shell + shells - k, shells)
        if k > 0:
            head_copy(k).wait_recv()
        part = heads_ref[shell, 0:dirs, :]
        woven[0:dirs, 0:coeffs] = part
        woven[dirs:2 * dirs, coeffs:2 * coeffs] = part

        def send(step, carry):
            space = lax.rem(me_space + step, spaces)
            block = feat_ref[pl.ds(pl.multiple_of(space * rows, rows), rows), :]
            value = lax.dot_general(
                block, woven[...], (((1,), (1,)), ((), ())), precision=HIGH,
                preferred_element_type=jnp.float32,
            )
            at = space * shells + shell
            sent[at, 0:rows, :] = value
            sent[at, rows:rows + EXTRA, :] = small_ref[space]
            copy_to(space, shell).start()
            return carry

        if k == 0:
            value = lax.dot_general(
                feat_ref[pl.ds(pl.multiple_of(me_space * rows, rows), rows), :], woven[...],
                (((1,), (1,)), ((), ())), precision=HIGH, preferred_element_type=jnp.float32,
            )
            pairs_ref[me, 0:rows, :] = value
            pairs_ref[me, rows:rows + EXTRA, :] = small_ref[me_space]
        lax.fori_loop(1 if k == 0 else 0, spaces, send, 0)

    def finish(k, carry):
        other = lax.rem(me + k, total)
        space, shell = lax.div(other, shells), lax.rem(other, shells)
        copy_to(space, shell).wait_send()
        pltpu.make_async_remote_copy(
            src_ref=sent.at[other], dst_ref=pairs_ref.at[other],
            send_sem=send_sem.at[other], recv_sem=recv_sem.at[other],
            device_id=(space, shell), device_id_type=MESH,
        ).wait_recv()
        return carry

    lax.fori_loop(1, total, finish, 0)
    for k in range(1, shells):
        head_copy(k).wait_send()


def exchange(spaces, shells, feat_pairs, head, small):
    rows = feat_pairs.shape[0] // spaces
    dirs = head.shape[0] - 2 * spaces
    total = spaces * shells
    vmem = pl.BlockSpec(memory_space=pltpu.VMEM)
    out = (total, rows + EXTRA, 2 * dirs)
    return pl.pallas_call(
        functools.partial(exchange_kernel, spaces, shells),
        out_shape=(
            jax.ShapeDtypeStruct(out, jnp.float32),
            jax.ShapeDtypeStruct((shells,) + head.shape, jnp.float32),
        ),
        in_specs=[vmem] * 3,
        out_specs=(vmem, vmem),
        scratch_shapes=[
            pltpu.VMEM(out, jnp.float32),
            pltpu.VMEM((2 * dirs, feat_pairs.shape[1]), jnp.float32),
            pltpu.SemaphoreType.DMA((total,)),
            pltpu.SemaphoreType.DMA((total,)),
            pltpu.SemaphoreType.DMA((shells,)),
            pltpu.SemaphoreType.DMA((shells,)),
        ],
        compiler_params=pltpu.CompilerParams(
            collective_id=0, has_side_effects=True, vmem_limit_bytes=56 * 1024 * 1024
        ),
    )(feat_pairs, head, small)


def message_kernel(spaces, shells, shared, from_ref, to_ref, send_sem, recv_sem):
    me_space, me_shell = lax.axis_index("space"), lax.axis_index("shell")
    me = me_space * shells + me_shell
    total = spaces * shells
    greet_all(spaces, shells, me_space, me_shell)

    def source(at):
        return lax.div(at, shells) if shared else at

    def copy_of(other, slot):
        return pltpu.make_async_remote_copy(
            src_ref=from_ref.at[source(other)], dst_ref=to_ref.at[slot],
            send_sem=send_sem.at[other], recv_sem=recv_sem.at[slot],
            device_id=(lax.div(other, shells), lax.rem(other, shells)), device_id_type=MESH,
        )

    def send(k, carry):
        copy_of(lax.rem(me + k, total), me).start()
        return carry

    lax.fori_loop(1, total, send, 0)
    to_ref[me] = from_ref[source(me)]

    def finish(k, carry):
        other = lax.rem(me + k, total)
        copy_of(other, me).wait_send()
        copy_of(other, other).wait_recv()
        return carry

    lax.fori_loop(1, total, finish, 0)


def message(spaces, shells, shared, values):
    total = spaces * shells
    vmem = pl.BlockSpec(memory_space=pltpu.VMEM)
    return pl.pallas_call(
        functools.partial(message_kernel, spaces, shells, shared),
        out_shape=jax.ShapeDtypeStruct((total,) + values.shape[1:], jnp.float32),
        in_specs=[vmem],
        out_specs=vmem,
        scratch_shapes=[pltpu.SemaphoreType.DMA((total,)), pltpu.SemaphoreType.DMA((total,))],
        compiler_params=pltpu.CompilerParams(
            collective_id=2 if shared else 1, has_side_effects=True
        ),
    )(values)


def on_device(spaces, shells, weights, seg_streamline, seg_features, pair_counts, seg_voxel, dictionary,
              measured):
    blocks = seg_streamline.shape[2]
    slots = seg_streamline.shape[3]
    coeffs = seg_features.shape[4]
    rows = slots // 2
    dirs = dictionary.shape[1]
    streams = weights.shape[0]
    counts = pair_counts.reshape(blocks)

    owner = seg_streamline.reshape(blocks, rows, 2).transpose(0, 2, 1).reshape(-1)
    voxel = seg_voxel.reshape(blocks, rows, 2).transpose(0, 2, 1).reshape(blocks, slots)
    head = jnp.concatenate(
        [dictionary.T, voxel.reshape(2 * blocks, rows).astype(jnp.float32)], axis=0
    )

    live = lax.broadcasted_iota(jnp.int32, (blocks, slots), 1) < counts[:, None]
    masked = jnp.where(
        live[:, :, None], seg_features.reshape(blocks, slots, coeffs), jnp.float32(0.0)
    )
    feat_pairs = masked.reshape(blocks * rows, 2 * coeffs)
    sq = jnp.sum((masked * masked).reshape(blocks, rows, 2, coeffs), axis=3)
    sq = sq.transpose(0, 2, 1).reshape(-1)

    hi = (owner // LANES)[:, None] == lax.broadcasted_iota(jnp.int32, (1, streams // LANES), 1)
    lo = (owner % LANES)[:, None] == lax.broadcasted_iota(jnp.int32, (1, LANES), 1)
    hi = hi.astype(jnp.float32)

    def pick(table):
        wide = jnp.dot(hi, table, precision=HIGH)
        return jnp.sum(jnp.where(lo, wide, 0.0), axis=1)

    def add_up(values):
        return lax.dot_general(
            hi, jnp.where(lo, values[:, None], 0.0), (((0,), (0,)), ((), ())), precision=HIGH
        )

    scaling = 0.5 / (0.5 + add_up(sq))

    current = weights.reshape(streams // LANES, LANES)
    extra = jnp.broadcast_to(counts[:, None, None].astype(jnp.float32), (blocks, EXTRA - 2, rows))
    small = jnp.concatenate([pick(current).reshape(blocks, 2, rows), extra], axis=1)
    pairs, heads = exchange(spaces, shells, feat_pairs, head, small)
    voxel_all = heads[:, dirs:, :].astype(jnp.int32).reshape(shells, blocks, slots)
    voxel_all = voxel_all.transpose(1, 0, 2).reshape(-1)
    x_slots = pairs[:, rows:rows + 2, :]
    counts_all = pairs[:, rows + 2, 0].astype(jnp.int32)

    start = jnp.concatenate([-measured.T, jnp.zeros_like(measured).T], axis=1)

    for iteration in range(ITERS):
        resid, grads = local_step(voxel_all, x_slots, counts_all, pairs, start, dirs)
        back = message(spaces, shells, False, grads)
        slot_grad = jnp.sum(back.reshape(blocks, shells, 2, rows), axis=1)
        current = jnp.maximum(current - scaling * add_up(slot_grad.reshape(-1)), 0.0)
        if iteration < ITERS - 1:
            x_slots = message(spaces, shells, True, pick(current).reshape(blocks, 2, rows))
    return current.reshape(streams), resid[:, :dirs].T


def solution(mesh):
    in_specs = (
        P(("space", "shell")),
        P("space", "shell", None, None),
        P("space", "shell", None, None, None),
        P("space", "shell", None),
        P("space", "shell", None, None),
        P(None, "shell"),
        P("shell", "space"),
    )
    out_specs = (P(("space", "shell")), P("shell", "space"))
    return jax.shard_map(
        functools.partial(on_device, mesh.shape["space"], mesh.shape["shell"]),
        mesh=mesh, in_specs=in_specs, out_specs=out_specs, check_vma=False,
    )
```
